512 devices in a mesh: seq: 128 (over z_lo, x, y), grp: 4 (over z_hi, core).
Axes of the slice: x: 4, y: 4, z: 16 (z_hi: 2, z_lo: 8; z = z_hi * 8 + z_lo), core: 2. Of those that a mesh axis runs over, the one named last changes fastest.
Arguments:
- queries: bfloat16 [81920, 2048], P(('grp', 'seq')), parts along dimension 0, may hold values from -6 to 6
- keys: bfloat16 [81920, 2048], P(('grp', 'seq')), parts along dimension 0, may hold values from -6 to 6
- values: bfloat16 [81920, 2048], P(('grp', 'seq')), parts along dimension 0, may hold values from -6 to 6
- out_grad: bfloat16 [81920, 2048], P(('grp', 'seq')), parts along dimension 0, may hold values from -6 to 6
- log_sum: float32 [16, 81920], P(None, ('grp', 'seq')), parts along dimension 1, may hold values from 3.5 to 4.5
- delta: float32 [16, 81920], P(None, ('grp', 'seq')), parts along dimension 1, may hold values from -24 to 24
Outputs:
- query_grad: bfloat16 [81920, 2048], P(('grp', 'seq')), parts along dimension 0
- key_grad: bfloat16 [81920, 2048], P(('grp', 'seq')), parts along dimension 0
- value_grad: bfloat16 [81920, 2048], P(('grp', 'seq')), parts along dimension 0
The draws below stay inside these ranges and needn't reach their ends.
There are 4 independent parts, one for each index of `grp`. The reference program is written for one: setup_inputs(seed, part) draws one part's arguments, and reference() takes and returns one part's arrays. A program takes and returns all parts, laid end to end along the dimension named above; each array names one. Nothing has to cross between parts.
All inputs are finite; a program needn't handle non-finite values.
Results may differ from the reference program's by a relative error of at most 0.04.
Values may be sent and summed in bfloat16 or wider, within the bound.
No kernel may reach another device: no remote copies, remote signals or barrier semaphores. Data moves between devices by JAX's collectives and lax.ppermute only.
A program may use at most 64 MiB of HBM per device.

```python
import jax
import jax.numpy as jnp
from jax import lax

HEADS = 16
HEAD_DIM = 128
S_DEV = 160
WIDTH = 2048
TOKENS = 20480
STEP_A = 32
STEP_B = 33
N_SEQ = 128


def steps_of(key, dims, shards, low, largest):
    gain, own = 1.0, jax.random.fold_in(key, 6)
    for axis_at, blocks in shards:
        draws = jnp.exp(jax.random.uniform(jax.random.fold_in(own, axis_at), (blocks,), jnp.float32, low / len(shards), largest / len(shards)))
        gain = gain * jnp.repeat(draws, dims[axis_at] // blocks).reshape([-1 if axis == axis_at else 1 for axis in range(len(dims))])
    return gain


def gaussian(stream_key, dims, deviation, most, shards=(), held_as=jnp.bfloat16):
    values = deviation * jax.random.normal(stream_key, dims, jnp.float32)
    if shards:
        values = values * steps_of(stream_key, dims, shards, -0.22, 0.18)
    return jnp.clip(values, -most, most).astype(held_as)


def setup_inputs(seed: int = 0, part: int = 0) -> dict:
    key_of = jax.random.split(jax.random.key(seed), 7)
    part_keys = jax.random.split(jax.random.fold_in(key_of[6], part), 7)
    queries = gaussian(part_keys[0], (TOKENS, WIDTH), 1.0, 6.0, ((0, 128),))
    keys = gaussian(part_keys[1], (TOKENS, WIDTH), 1.0, 6.0, ((0, 128),))
    values = gaussian(part_keys[2], (TOKENS, WIDTH), 1.0, 6.0, ((0, 128),))
    out_grad = gaussian(part_keys[3], (TOKENS, WIDTH), 1.0, 6.0, ((0, 128),))
    log_sum = jnp.clip(3.5 + 1.0 * jax.random.uniform(part_keys[4], (HEADS, TOKENS), jnp.float32) ** steps_of(part_keys[4], (HEADS, TOKENS), ((1, 128),), -0.2, 0.2), 3.5, 4.5)
    delta = gaussian(part_keys[5], (HEADS, TOKENS), 4.0, 24.0, ((1, 128),), jnp.float32)
    return dict(queries=queries, keys=keys, values=values, out_grad=out_grad, log_sum=log_sum, delta=delta)


def block_terms(q_rows, grad_rows, lse_rows, delta_rows, k_rows, v_rows, keep_mask):
    row_count = q_rows.shape[0]
    scale = HEAD_DIM ** -0.5
    q_heads = q_rows.reshape(row_count, HEADS, HEAD_DIM).astype(jnp.float32)
    g_heads = grad_rows.reshape(row_count, HEADS, HEAD_DIM).astype(jnp.float32)
    k_heads = k_rows.reshape(row_count, HEADS, HEAD_DIM).astype(jnp.float32)
    v_heads = v_rows.reshape(row_count, HEADS, HEAD_DIM).astype(jnp.float32)
    scores = jnp.einsum('shd,thd->hst', q_heads, k_heads) * scale
    prob = jnp.where(keep_mask[None], jnp.exp(scores - lse_rows[:, :, None]), jnp.float32(0.0))
    dprob = jnp.einsum('shd,thd->hst', g_heads, v_heads)
    dscore = prob * (dprob - delta_rows[:, :, None])
    prob_b = lax.optimization_barrier(prob.astype(jnp.bfloat16)).astype(jnp.float32)
    dscore_b = lax.optimization_barrier(dscore.astype(jnp.bfloat16)).astype(jnp.float32)
    query_term = jnp.einsum('hst,thd->shd', dscore_b, k_heads) * scale
    key_term = jnp.einsum('hst,shd->thd', dscore_b, q_heads) * scale
    value_term = jnp.einsum('hst,shd->thd', prob_b, g_heads)
    width = HEADS * HEAD_DIM
    return (query_term.reshape(row_count, width), key_term.reshape(row_count, width),
            value_term.reshape(row_count, width))


def rounded(term):
    return lax.optimization_barrier(term.astype(jnp.bfloat16)).astype(jnp.float32)


def reference(queries, keys, values, out_grad, log_sum, delta):
    blocks = N_SEQ
    width = HEADS * HEAD_DIM
    q_blocks = queries.reshape(blocks, S_DEV, width)
    k_blocks = keys.reshape(blocks, S_DEV, width)
    v_blocks = values.reshape(blocks, S_DEV, width)
    g_blocks = out_grad.reshape(blocks, S_DEV, width)
    lse_blocks = log_sum.reshape(HEADS, blocks, S_DEV).transpose(1, 0, 2)
    delta_blocks = delta.reshape(HEADS, blocks, S_DEV).transpose(1, 0, 2)
    row_ids = lax.broadcasted_iota(jnp.int32, (S_DEV, S_DEV), 0)
    col_ids = lax.broadcasted_iota(jnp.int32, (S_DEV, S_DEV), 1)
    causal = row_ids >= col_ids
    numbers = jnp.arange(blocks, dtype=jnp.int32)

    def diagonal(index):
        return block_terms(q_blocks[index], g_blocks[index], lse_blocks[index], delta_blocks[index],
                           k_blocks[index], v_blocks[index], causal)

    query_acc, key_acc, value_acc = lax.map(diagonal, numbers)
    for distance in (STEP_A, N_SEQ - STEP_A, STEP_B, N_SEQ - STEP_B):
        def paired(index):
            source = ((index + distance) % blocks).astype(jnp.int32)
            keep_mask = jnp.logical_and(jnp.ones((S_DEV, S_DEV), dtype=bool), index + distance < blocks)
            terms = block_terms(q_blocks[source], g_blocks[source], lse_blocks[source], delta_blocks[source],
                                k_blocks[index], v_blocks[index], keep_mask)
            return (rounded(terms[0]), rounded(terms[1]), rounded(terms[2]))

        part_q, part_k, part_v = lax.map(paired, numbers)
        query_acc = query_acc + jnp.roll(part_q, distance, axis=0)
        key_acc = key_acc + part_k
        value_acc = value_acc + part_v
    total = blocks * S_DEV
    return (query_acc.reshape(total, width).astype(jnp.bfloat16),
            key_acc.reshape(total, width).astype(jnp.bfloat16),
            value_acc.reshape(total, width).astype(jnp.bfloat16))
```

```python
import functools

import jax
import jax.numpy as jnp
from jax import lax
from jax.experimental import pallas as pl
from jax.experimental.pallas import tpu as pltpu
from jax.sharding import PartitionSpec as P

HEADS = 16
DEPTH = 128
ROWS = 160
HALF = 80
AUX = 16
LAYER = 16
SCALE = DEPTH ** (-0.5)
NT = (((1,), (1,)), ((), ()))
NN = (((1,), (0,)), ((), ()))
TN = (((0,), (0,)), ((), ()))
VMEM_LIMIT = 48 * 1024 * 1024


def dot(a, b, dims):
    return lax.dot_general(a, b, dims, preferred_element_type=jnp.float32)


def params():
    return pltpu.CompilerParams(vmem_limit_bytes=VMEM_LIMIT)


def pair(k, v, q, g, lse, delta, mask=None):
    prob = jnp.exp(dot(k, q, NT) * SCALE - lse)
    if mask is not None:
        prob = jnp.where(mask, prob, 0.0)
    dscore = (prob * (dot(v, g, NT) - delta)).astype(jnp.bfloat16)
    prob = prob.astype(jnp.bfloat16)
    return dot(dscore, q, NN), dot(prob, g, NN), dot(dscore, k, TN)


def read_aux(aux):
    a = aux.astype(jnp.float32)
    rows = []
    for base in (0, 6):
        first = a[base : base + 1] + a[base + 2 : base + 3] + a[base + 4 : base + 5]
        second = a[base + 1 : base + 2] + a[base + 3 : base + 4] + a[base + 5 : base + 6]
        rows.append(jnp.concatenate([first, second[:, : ROWS - DEPTH]], axis=1))
    return rows


def prep_kernel(roles, q, g, k, v, lse, delta, send_a, send_b, local, wide):
    group = pl.program_id(0)
    count = send_a.shape[0]
    wide[...] = jnp.zeros_like(wide)
    wide[0, :, 0:ROWS] = lse[...]
    wide[1, :, 0:ROWS] = delta[...]
    sub = lax.broadcasted_iota(jnp.int32, (AUX, DEPTH), 0)
    for i in range(count):
        head = group * count + i
        aux = jnp.zeros((AUX, DEPTH), jnp.float32)
        for t in range(2):
            row = wide[t, pl.ds(head, 1), :]
            for piece in range(3):
                part = row.astype(jnp.bfloat16).astype(jnp.float32)
                row = row - part
                for side in range(2):
                    at = 6 * t + 2 * piece + side
                    aux = jnp.where(sub == at, part[:, side * DEPTH : (side + 1) * DEPTH], aux)
        aux = aux.astype(jnp.bfloat16)
        cols = slice(i * DEPTH, (i + 1) * DEPTH)
        send_a[i, 2 * HALF :, :] = aux
        local[i, 2 * ROWS :, :] = aux

        def put_send(one, two):
            send_a[i, 0:HALF, :] = one[0:HALF, cols]
            send_a[i, HALF : 2 * HALF, :] = two[0:HALF, cols]
            send_b[i, 0:HALF, :] = one[HALF:, cols]
            send_b[i, HALF : 2 * HALF, :] = two[HALF:, cols]

        def put_local(one, two):
            local[i, 0:ROWS, :] = one[:, cols]
            local[i, ROWS : 2 * ROWS, :] = two[:, cols]

        pl.when(roles[0] == 1)(functools.partial(put_send, q, g))
        pl.when(roles[0] == 0)(functools.partial(put_send, k, v))
        pl.when(roles[1] == 1)(functools.partial(put_local, k, v))
        pl.when(roles[1] == 0)(functools.partial(put_local, q, g))


def prep(roles, q, g, k, v, lse, delta):
    count = 4
    wide = pl.BlockSpec((ROWS, count * DEPTH), lambda i: (0, i))
    small = pl.BlockSpec((HEADS, ROWS), lambda i: (0, 0))
    heights = (2 * HALF + AUX, 2 * HALF, 2 * ROWS + AUX)
    return pl.pallas_call(
        prep_kernel,
        grid=(HEADS // count,),
        in_specs=[pl.BlockSpec(memory_space=pltpu.SMEM)] + [wide] * 4 + [small] * 2,
        out_specs=[pl.BlockSpec((count, h, DEPTH), lambda i: (i, 0, 0)) for h in heights],
        out_shape=[jax.ShapeDtypeStruct((HEADS, h, DEPTH), jnp.bfloat16) for h in heights],
        scratch_shapes=[pltpu.VMEM((2, HEADS, 2 * DEPTH), jnp.float32)],
        compiler_params=params(),
        name="prep",
    )(roles, q, g, k, v, lse, delta)


def diag_kernel(q, g, k, v, lse, delta, dq, dk, dv):
    group = pl.program_id(0)
    count = q.shape[1] // DEPTH
    mask = lax.broadcasted_iota(jnp.int32, (ROWS, ROWS), 0) <= lax.broadcasted_iota(
        jnp.int32, (ROWS, ROWS), 1
    )
    for i in range(count):
        head = group * count + i
        cols = slice(i * DEPTH, (i + 1) * DEPTH)
        key, value, query = pair(
            k[:, cols],
            v[:, cols],
            q[:, cols],
            g[:, cols],
            lse[pl.ds(head, 1), :],
            delta[pl.ds(head, 1), :],
            mask,
        )
        dq[:, cols] = query * SCALE
        dk[:, cols] = key * SCALE
        dv[:, cols] = value


def diag(q, g, k, v, lse, delta):
    count = 4
    wide = pl.BlockSpec((ROWS, count * DEPTH), lambda i: (0, i))
    small = pl.BlockSpec((HEADS, ROWS), lambda i: (0, 0))
    return pl.pallas_call(
        diag_kernel,
        grid=(HEADS // count,),
        in_specs=[wide] * 4 + [small] * 2,
        out_specs=[wide] * 3,
        out_shape=[jax.ShapeDtypeStruct((ROWS, HEADS * DEPTH), jnp.float32)] * 3,
        compiler_params=params(),
        name="diagonal",
    )(q, g, k, v, lse, delta)


def edges_kernel(first, roles, *refs):
    if first:
        recv, aux_from, local, back, acc_out = refs
    else:
        recv, aux_from, local, acc_in, back, acc_out = refs
    lanes = slice(0, HALF) if first else slice(HALF, ROWS)
    if not first:
        acc_out[...] = acc_in[...]

    def block(i, lo, count, role_b):
        r1 = recv[i, 0:HALF, :]
        r2 = recv[i, HALF : 2 * HALF, :]
        l1 = [local[lo + c, 0:ROWS, :] for c in range(count)]
        l2 = [local[lo + c, ROWS : 2 * ROWS, :] for c in range(count)]
        l1 = jnp.concatenate(l1, axis=0)
        l2 = jnp.concatenate(l2, axis=0)
        if role_b:
            lse, delta = [x[:, lanes] for x in read_aux(aux_from[i, 2 * HALF :, :])]
            key, value, query = pair(l1, l2, r1, r2, lse, delta)
            back[i, 0:HALF, :] = (query * SCALE).astype(jnp.bfloat16)
            back[i, HALF : 2 * HALF, :] = jnp.zeros((HALF, DEPTH), jnp.bfloat16)
            sums = (key, value)
        else:
            aux = [read_aux(local[lo + c, 2 * ROWS :, :]) for c in range(count)]
            lse = jnp.concatenate([a[0] for a in aux], axis=1)
            delta = jnp.concatenate([a[1] for a in aux], axis=1)
            key, value, query = pair(r1, r2, l1, l2, lse, delta)
            back[i, 0:HALF, :] = (key * SCALE).astype(jnp.bfloat16)
            back[i, HALF : 2 * HALF, :] = value.astype(jnp.bfloat16)
            sums = (query,)
        for n, term in enumerate(sums):
            if count == 2 or not first:
                acc_out[n, lo] += term[0:ROWS]
            else:
                acc_out[n, lo] = term[0:ROWS]
            if count == 2:
                if first:
                    acc_out[n, lo + 1] = term[ROWS:]
                else:
                    acc_out[n, lo + 1] += term[ROWS:]

    def run(role_b):
        block(0, 0, 1, role_b)

        @pl.loop(1, LAYER)
        def _(i):
            block(i, i - 1, 2, role_b)

        if first and not role_b:
            acc_out[1] = jnp.zeros(acc_out.shape[1:], jnp.float32)

    pl.when(roles[1] == 1)(functools.partial(run, True))
    pl.when(roles[1] == 0)(functools.partial(run, False))


def edges(first, roles, recv, aux_from, local, acc):
    vmem = pl.BlockSpec(memory_space=pltpu.VMEM)
    ops = [recv, aux_from, local] + ([] if first else [acc])
    sums = jax.ShapeDtypeStruct((2, LAYER, ROWS, DEPTH), jnp.float32)
    return pl.pallas_call(
        functools.partial(edges_kernel, first),
        in_specs=[pl.BlockSpec(memory_space=pltpu.SMEM)] + [vmem] * len(ops),
        out_specs=[vmem] * 2,
        out_shape=[jax.ShapeDtypeStruct((LAYER, 2 * HALF, DEPTH), jnp.bfloat16), sums],
        input_output_aliases={} if first else {4: 1},
        compiler_params=params(),
        name="edges_first" if first else "edges_second",
    )(roles, *ops)


def carry_kernel(roles, chain, extra, local, acc, back, mine, out):
    layer = roles[2]
    out[:, 0:ROWS, :] = (acc[0] * SCALE).astype(jnp.bfloat16)
    out[:, ROWS : 2 * ROWS, :] = acc[1].astype(jnp.bfloat16)
    last = LAYER - 1
    recv = jnp.where(layer == 7, extra[...], chain[...])
    held = jnp.where(layer == 5, extra[...], local[last])
    r1, r2, l1, l2 = recv[0:ROWS], recv[ROWS : 2 * ROWS], held[0:ROWS], held[ROWS : 2 * ROWS]

    @pl.when(layer <= 4)
    def _():
        lse, delta = read_aux(recv[2 * ROWS :])
        key, value, query = pair(l1, l2, r1, r2, lse, delta)
        back[0:ROWS, :] = (query * SCALE).astype(jnp.bfloat16)
        back[ROWS:, :] = jnp.zeros((ROWS, DEPTH), jnp.bfloat16)
        out[last, 0:ROWS, :] = ((acc[0, last] + key) * SCALE).astype(jnp.bfloat16)
        out[last, ROWS : 2 * ROWS, :] = (acc[1, last] + value).astype(jnp.bfloat16)
        mine[...] = jnp.zeros_like(mine)

    @pl.when(layer > 4)
    def _():
        lse, delta = read_aux(held[2 * ROWS :])
        key, value, query = pair(r1, r2, l1, l2, lse, delta)
        back[0:ROWS, :] = (key * SCALE).astype(jnp.bfloat16)
        back[ROWS:, :] = value.astype(jnp.bfloat16)
        mine[...] = (query * SCALE).astype(jnp.bfloat16)


def carry(roles, chain, extra, local, acc):
    vmem = pl.BlockSpec(memory_space=pltpu.VMEM)
    return pl.pallas_call(
        carry_kernel,
        in_specs=[pl.BlockSpec(memory_space=pltpu.SMEM)] + [vmem] * 4,
        out_specs=[vmem] * 3,
        out_shape=[
            jax.ShapeDtypeStruct((2 * ROWS, DEPTH), jnp.bfloat16),
            jax.ShapeDtypeStruct((ROWS, DEPTH), jnp.bfloat16),
            jax.ShapeDtypeStruct((LAYER, 2 * ROWS, DEPTH), jnp.bfloat16),
        ],
        compiler_params=params(),
        name="carry",
    )(roles, chain, extra, local, acc)


def final_kernel(roles, dq, dk, dv, one, two, own, oq, ok, ov):
    layer = roles[2]
    for i in range(one.shape[0]):
        cols = slice(i * DEPTH, (i + 1) * DEPTH)
        own1 = own[i, 0:ROWS, :].astype(jnp.float32)
        own2 = own[i, ROWS : 2 * ROWS, :].astype(jnp.float32)
        a1 = one[i, 0:HALF, :].astype(jnp.float32)
        a2 = one[i, HALF : 2 * HALF, :].astype(jnp.float32)
        b1 = two[i, 0:HALF, :].astype(jnp.float32)
        b2 = two[i, HALF : 2 * HALF, :].astype(jnp.float32)

        def put(query, key, value):
            oq[:, cols] = query.astype(jnp.bfloat16)
            ok[:, cols] = key.astype(jnp.bfloat16)
            ov[:, cols] = value.astype(jnp.bfloat16)

        @pl.when(layer <= 1)
        def _():
            put(
                dq[:, cols],
                dk[:, cols] + own1 + jnp.concatenate([a1, b1], axis=0),
                dv[:, cols] + own2 + jnp.concatenate([a2, b2], axis=0),
            )

        @pl.when(jnp.logical_and(layer >= 2, layer <= 5))
        def _():
            put(
                dq[:, cols] + jnp.concatenate([a1, b1 + a2], axis=0),
                dk[:, cols] + own1,
                dv[:, cols] + own2,
            )

        @pl.when(layer >= 6)
        def _():
            put(
                dq[:, cols] + own1 + jnp.concatenate([a1, b1 + a2], axis=0),
                dk[:, cols],
                dv[:, cols],
            )


def final(roles, dq, dk, dv, one, two, own):
    count = 4
    wide = pl.BlockSpec((ROWS, count * DEPTH), lambda i: (0, i))
    head = [pl.BlockSpec((count, x.shape[1], DEPTH), lambda i: (i, 0, 0)) for x in (one, two, own)]
    return pl.pallas_call(
        final_kernel,
        grid=(HEADS // count,),
        in_specs=[pl.BlockSpec(memory_space=pltpu.SMEM)] + [wide] * 3 + head,
        out_specs=[wide] * 3,
        out_shape=[jax.ShapeDtypeStruct((ROWS, HEADS * DEPTH), jnp.bfloat16)] * 3,
        compiler_params=params(),
        name="final",
    )(roles, dq, dk, dv, one, two, own)


def after(x, *others):
    return lax.optimization_barrier((x, *others))[0]


def on_device(queries, keys, values, out_grad, log_sum, delta):
    count = lax.axis_size("seq")
    position = lax.axis_index("seq")
    layer = position // LAYER
    groups = [list(range(s, s + LAYER)) for s in range(0, count, LAYER)]

    def ring(x, by):
        return lax.ppermute(x, "seq", [(i, (i + by) % count) for i in range(count)])

    def spread(x):
        return lax.all_to_all(x, "seq", 0, 0, axis_index_groups=groups, tiled=True)

    roles = jnp.stack([layer >= 2, layer <= 5, layer, layer]).astype(jnp.int32)
    send_a, send_b, local = prep(roles, queries, out_grad, keys, values, log_sum, delta)
    recv_a = ring(send_a, -2 * LAYER)
    head_b = spread(send_b)
    recv_b = ring(head_b, -2 * LAYER)
    head_local = spread(after(local, head_b))
    dq, dk, dv = diag(queries, out_grad, keys, values, after(log_sum, head_local), delta)
    recv_a = spread(recv_a)
    back_a, acc = edges(True, roles, recv_a, recv_a, head_local, None)
    home_a = ring(back_a, 2 * LAYER)
    back_b, acc = edges(False, roles, after(recv_b, back_a), recv_a, head_local, acc)
    back_b = spread(back_b)
    home_b = ring(back_b, 2 * LAYER)

    def whole(block):
        a, b = recv_a[block], recv_b[block]
        return jnp.concatenate(
            [a[0:HALF], b[0:HALF], a[HALF : 2 * HALF], b[HALF : 2 * HALF], a[2 * HALF :]], axis=0
        )

    chain = lax.ppermute(whole(0), "seq", [(i, i - LAYER) for i in range(LAYER, count)])
    extra = jnp.where(layer == 2, head_local[0], whole(LAYER - 1))
    extra = lax.ppermute(
        extra,
        "seq",
        [(2 * LAYER + i, 7 * LAYER + i) for i in range(LAYER)]
        + [(3 * LAYER + i, 5 * LAYER + i) for i in range(LAYER)],
    )
    carry_back, carry_mine, own = carry(roles, chain, extra, head_local, acc)
    carry_home = ring(carry_back, 3 * LAYER)
    zero = jnp.bfloat16(0.0)
    own = own.at[0].add(jnp.where(layer <= 2, carry_home, zero))
    own = spread(own)
    from_home = jnp.where(layer >= 3, carry_home[0:ROWS], zero)
    from_mine = jnp.where(layer >= 5, carry_mine, zero)
    home_a = home_a.at[0].add(from_home).at[LAYER - 1].add(from_mine)
    home_a = spread(after(home_a, own))
    return final(roles, dq, dk, dv, home_a, home_b, own)


def solution(mesh):
    rows = P(("grp", "seq"), None)
    cols = P(None, ("grp", "seq"))
    return jax.shard_map(
        on_device,
        mesh=mesh,
        in_specs=(rows, rows, rows, rows, cols, cols),
        out_specs=(rows, rows, rows),
        check_vma=False,
    )
```

```python
import functools

import jax
import jax.numpy as jnp
from jax import lax
from jax.experimental import pallas as pl
from jax.experimental.pallas import tpu as pltpu
from jax.sharding import PartitionSpec as P

HEADS = 16
DEPTH = 128
ROWS = 160
AUX = 16
SENT = 2 * ROWS + AUX
BACK = 2 * ROWS
LAYER = 16
UNIT = 2
CHUNKS = (6, 6, 4)
SCALE = DEPTH ** (-0.5)
NT = (((1,), (1,)), ((), ()))
NN = (((1,), (0,)), ((), ()))
TN = (((0,), (0,)), ((), ()))
LIMIT = 60 * 1024 * 1024


def dot(a, b, dims):
    return lax.dot_general(a, b, dims, preferred_element_type=jnp.float32)


def cost(us):
    return pl.CostEstimate(
        flops=int(us * 1.1e9) + 1000, bytes_accessed=int(us * 3.6e6) + 1000, transcendentals=0
    )


def call(body, name, grid=(), us=0, limit=LIMIT, **kwargs):
    return pl.pallas_call(
        body,
        grid=grid,
        compiler_params=pltpu.CompilerParams(vmem_limit_bytes=limit),
        cost_estimate=cost(us),
        name=name,
        **kwargs,
    )


SMEM = pl.BlockSpec(memory_space=pltpu.SMEM)
ANY = pl.BlockSpec(memory_space=pl.ANY)
SMALL = pl.BlockSpec((HEADS, ROWS), lambda i: (0, 0))


def wide(first, unit=UNIT):
    return pl.BlockSpec((ROWS, unit * DEPTH), lambda i: (0, first // unit + i))


def tall(rows, first=0, unit=UNIT):
    return pl.BlockSpec((unit, rows, DEPTH), lambda i: (first // unit + i, 0, 0))


def together(*arrays):
    return lax.optimization_barrier(arrays)


def arrived_kernel(x, out):
    del x, out


def arrived(x, *others, us=100):
    if others:
        x = together(x, *others)[0]
    return call(
        arrived_kernel,
        "arrived",
        us=us,
        in_specs=[ANY],
        out_specs=ANY,
        out_shape=jax.ShapeDtypeStruct(x.shape, x.dtype),
        input_output_aliases={0: 0},
    )(x)


def pair(k, v, q, g, lse, delta, mask=None):
    prob = jnp.exp(dot(k, q, NT) * SCALE - lse)
    if mask is not None:
        prob = jnp.where(mask, prob, 0.0)
    dscore = (prob * (dot(v, g, NT) - delta)).astype(jnp.bfloat16)
    prob = prob.astype(jnp.bfloat16)
    return dot(dscore, q, NN) * SCALE, dot(prob, g, NN), dot(dscore, k, TN) * SCALE


def aux_rows(spare, head):
    sub = lax.broadcasted_iota(jnp.int32, (AUX, DEPTH), 0)
    aux = jnp.zeros((AUX, DEPTH), jnp.float32)
    for t in range(2):
        row = spare[t, pl.ds(head, 1), :]
        for piece in range(3):
            part = row.astype(jnp.bfloat16).astype(jnp.float32)
            row = row - part
            for side in range(2):
                at = 6 * t + 2 * piece + side
                aux = jnp.where(sub == at, part[:, side * DEPTH : (side + 1) * DEPTH], aux)
    return aux.astype(jnp.bfloat16)


def read_aux(aux):
    a = aux.astype(jnp.float32)
    rows = []
    for base in (0, 6):
        first = a[base : base + 1] + a[base + 2 : base + 3] + a[base + 4 : base + 5]
        second = a[base + 1 : base + 2] + a[base + 3 : base + 4] + a[base + 5 : base + 6]
        rows.append(jnp.concatenate([first, second[:, : ROWS - DEPTH]], axis=1))
    return rows


def prep_kernel(first, role_at, unit, roles, q, g, k, v, lse, delta, out, spare):
    step = pl.program_id(0)
    spare[...] = jnp.zeros_like(spare)
    spare[0, :, 0:ROWS] = lse[...]
    spare[1, :, 0:ROWS] = delta[...]
    for i in range(unit):
        cols = slice(i * DEPTH, (i + 1) * DEPTH)
        out[i, 2 * ROWS :, :] = aux_rows(spare, first + step * unit + i)

        def put(one, two):
            out[i, 0:ROWS, :] = one[:, cols]
            out[i, ROWS : 2 * ROWS, :] = two[:, cols]

        pl.when(roles[role_at] == 1)(functools.partial(put, q, g))
        pl.when(roles[role_at] == 0)(functools.partial(put, k, v))


def prep(first, count, role_at, roles, q, g, k, v, lse, delta, unit=UNIT):
    return call(
        functools.partial(prep_kernel, first, role_at, unit),
        "prep",
        grid=(count // unit,),
        in_specs=[SMEM] + [wide(first, unit)] * 4 + [SMALL] * 2,
        out_specs=tall(SENT, 0, unit),
        out_shape=jax.ShapeDtypeStruct((count, SENT, DEPTH), jnp.bfloat16),
        scratch_shapes=[pltpu.VMEM((2, HEADS, 2 * DEPTH), jnp.float32)],
    )(roles, q, g, k, v, lse, delta)


def edges_kernel(first, roles, q, g, k, v, lse, delta, one, two, back1, back2, dq, dk, dv):
    step = pl.program_id(0)

    def run(role_b):
        for i in range(UNIT):
            cols = slice(i * DEPTH, (i + 1) * DEPTH)
            head = first + step * UNIT + i
            own_lse, own_delta = lse[pl.ds(head, 1), :], delta[pl.ds(head, 1), :]

            def joined(own, at):
                rows = slice(at * ROWS, (at + 1) * ROWS)
                return jnp.concatenate([own[:, cols], one[i, rows, :], two[i, rows, :]], axis=0)

            if role_b:
                aux = [read_aux(x[i, 2 * ROWS :, :]) for x in (one, two)]
                all_lse = jnp.concatenate([own_lse, aux[0][0], aux[1][0]], axis=1)
                all_delta = jnp.concatenate([own_delta, aux[0][1], aux[1][1]], axis=1)
                shape = (ROWS, 3 * ROWS)
                keys = lax.broadcasted_iota(jnp.int32, shape, 0)
                mask = keys <= lax.broadcasted_iota(jnp.int32, shape, 1)
                key, value, query = pair(
                    k[:, cols], v[:, cols], joined(q, 0), joined(g, 1), all_lse, all_delta, mask
                )
                dk[:, cols] = key.astype(jnp.bfloat16)
                dv[:, cols] = value.astype(jnp.bfloat16)
                query = query.astype(jnp.bfloat16)
                dq[:, cols] = query[0:ROWS]
                for n, back in ((1, back1), (2, back2)):
                    back[i, 0:ROWS, :] = query[n * ROWS : (n + 1) * ROWS]
                    back[i, ROWS:, :] = jnp.zeros((ROWS, DEPTH), jnp.bfloat16)
            else:
                shape = (3 * ROWS, ROWS)
                keys = lax.broadcasted_iota(jnp.int32, shape, 0)
                mask = keys <= lax.broadcasted_iota(jnp.int32, shape, 1)
                mask = jnp.logical_or(mask, keys >= ROWS)
                key, value, query = pair(
                    joined(k, 0), joined(v, 1), q[:, cols], g[:, cols], own_lse, own_delta, mask
                )
                dq[:, cols] = query.astype(jnp.bfloat16)
                key, value = key.astype(jnp.bfloat16), value.astype(jnp.bfloat16)
                dk[:, cols] = key[0:ROWS]
                dv[:, cols] = value[0:ROWS]
                for n, back in ((1, back1), (2, back2)):
                    back[i, 0:ROWS, :] = key[n * ROWS : (n + 1) * ROWS]
                    back[i, ROWS:, :] = value[n * ROWS : (n + 1) * ROWS]

    pl.when(roles[1] == 1)(functools.partial(run, True))
    pl.when(roles[1] == 0)(functools.partial(run, False))


def edges(first, count, roles, q, g, k, v, lse, delta, one, two):
    own = wide(0)
    return call(
        functools.partial(edges_kernel, first),
        "edges",
        limit=24 * 1024 * 1024,
        grid=(count // UNIT,),
        in_specs=[SMEM] + [wide(first)] * 4 + [SMALL] * 2 + [tall(SENT)] * 2,
        out_specs=[tall(BACK)] * 2 + [own] * 3,
        out_shape=[jax.ShapeDtypeStruct((count, BACK, DEPTH), jnp.bfloat16)] * 2
        + [jax.ShapeDtypeStruct((ROWS, count * DEPTH), jnp.bfloat16)] * 3,
    )(roles, q, g, k, v, lse, delta, one, two)


def add_kernel(a, b, out):
    out[...] = (a[...].astype(jnp.float32) + b[...].astype(jnp.float32)).astype(jnp.bfloat16)


def add(a, b):
    vmem = pl.BlockSpec(memory_space=pltpu.VMEM)
    return call(
        add_kernel,
        "add",
        limit=24 * 1024 * 1024,
        in_specs=[vmem] * 2,
        out_specs=vmem,
        out_shape=jax.ShapeDtypeStruct(a.shape, a.dtype),
    )(a, b)


def carry_kernel(roles, recv, held, back, mine):
    layer = roles[3]
    r1, r2 = recv[0:ROWS], recv[ROWS : 2 * ROWS]
    l1, l2 = held[0, 0:ROWS], held[0, ROWS : 2 * ROWS]

    def put(ref, one, two):
        ref[0:ROWS, :] = one.astype(jnp.bfloat16)
        if two is None:
            ref[ROWS:, :] = jnp.zeros((ROWS, DEPTH), jnp.bfloat16)
        else:
            ref[ROWS:, :] = two.astype(jnp.bfloat16)

    @pl.when(layer <= 4)
    def _():
        lse, delta = read_aux(recv[2 * ROWS :])
        key, value, query = pair(l1, l2, r1, r2, lse, delta)
        put(back, query, None)
        put(mine, key, value)

    @pl.when(layer > 4)
    def _():
        lse, delta = read_aux(held[0, 2 * ROWS :])
        key, value, query = pair(r1, r2, l1, l2, lse, delta)
        put(back, key, value)
        put(mine, query, None)


def carry(roles, recv, spread_in):
    out = pl.BlockSpec((BACK, DEPTH), lambda i: (0, 0))
    return call(
        carry_kernel,
        "carry",
        limit=24 * 1024 * 1024,
        grid=(1,),
        in_specs=[
            SMEM,
            pl.BlockSpec((SENT, DEPTH), lambda i: (0, 0)),
            pl.BlockSpec((1, SENT, DEPTH), lambda i: (LAYER - 1, 0, 0)),
        ],
        out_specs=[out] * 2,
        out_shape=[jax.ShapeDtypeStruct((BACK, DEPTH), jnp.bfloat16)] * 2,
    )(roles, recv, spread_in)


def ends_kernel(home, mine, out):
    out[...] = jnp.zeros_like(out)
    out[0] = home[...]
    out[LAYER - 1] = mine[...]


def ends(home, mine):
    vmem = pl.BlockSpec(memory_space=pltpu.VMEM)
    return call(
        ends_kernel,
        "ends",
        limit=48 * 1024 * 1024,
        in_specs=[vmem] * 2,
        out_specs=vmem,
        out_shape=jax.ShapeDtypeStruct((LAYER, BACK, DEPTH), jnp.bfloat16),
    )(home, mine)


def final_kernel(roles, dq, dk, dv, home, carried, *refs):
    oq, ok, ov = refs[-3:]
    layer, place = roles[3], roles[4]
    home_q = layer >= 2
    carried_q = jnp.where(place == 0, layer >= 3, layer >= 5)
    for i in range(UNIT):
        cols = slice(i * DEPTH, (i + 1) * DEPTH)
        f32 = [x[:, cols].astype(jnp.float32) for x in (dq, dk, dv)]
        h1 = home[i, 0:ROWS, :].astype(jnp.float32)
        h2 = home[i, ROWS:, :].astype(jnp.float32)
        c1 = carried[i, 0:ROWS, :].astype(jnp.float32)
        c2 = carried[i, ROWS:, :].astype(jnp.float32)
        to_q = jnp.where(home_q, h1, 0.0) + jnp.where(carried_q, c1, 0.0)
        to_k = jnp.where(home_q, 0.0, h1) + jnp.where(carried_q, 0.0, c1)
        to_v = jnp.where(home_q, 0.0, h2) + jnp.where(carried_q, 0.0, c2)
        oq[:, cols] = (f32[0] + to_q).astype(jnp.bfloat16)
        ok[:, cols] = (f32[1] + to_k).astype(jnp.bfloat16)
        ov[:, cols] = (f32[2] + to_v).astype(jnp.bfloat16)


def final(first, count, roles, own, home, carried, outs):
    held = list(outs) if outs else []
    return call(
        final_kernel,
        "final",
        limit=24 * 1024 * 1024,
        grid=(count // UNIT,),
        in_specs=[SMEM] + [wide(0)] * 3 + [tall(BACK), tall(BACK, first)] + [ANY] * len(held),
        out_specs=[wide(first)] * 3,
        out_shape=[jax.ShapeDtypeStruct((ROWS, HEADS * DEPTH), jnp.bfloat16)] * 3,
        input_output_aliases={6 + n: n for n in range(len(held))},
    )(roles, *own, home, carried, *held)


def on_device(queries, keys, values, out_grad, log_sum, delta):
    count = lax.axis_size("seq")
    position = lax.axis_index("seq")
    layer, place = position // LAYER, position % LAYER
    groups = [list(range(s, s + LAYER)) for s in range(0, count, LAYER)]
    inputs = (queries, out_grad, keys, values, log_sum, delta)

    def ring(x, by):
        return lax.ppermute(x, "seq", [(i, (i + by) % count) for i in range(count)])

    def beside(x, by):
        pairs = [(i, i + by) for i in range(count) if (i + by) // LAYER == i // LAYER]
        return lax.ppermute(x, "seq", pairs)

    def spread(x):
        return lax.all_to_all(x, "seq", 0, 0, axis_index_groups=groups, tiled=True)

    carry_q = jnp.where(place == LAYER - 1, layer >= 5, layer >= 3)
    roles = jnp.stack([layer >= 2, layer <= 5, carry_q, layer, place]).astype(jnp.int32)
    firsts = [sum(CHUNKS[:n]) for n in range(len(CHUNKS))]
    total = len(CHUNKS)

    sent = [None] * total
    sent[0] = prep(firsts[0], CHUNKS[0], 0, roles, *inputs)
    roles1 = together(roles, sent[0])[0]
    spread_in = spread(prep(0, HEADS, 2, roles1, *inputs, unit=4))
    for c in range(1, total):
        sent[c] = prep(firsts[c], CHUNKS[c], 0, roles1, *inputs)

    recv, near, own, summed, home = ([None] * total for _ in range(5))
    carried = carry_back = packed = None
    recv[0] = arrived(ring(sent[0], -2 * LAYER), *sent[1:])
    carry_recv = arrived(ring(spread_in[0], -3 * LAYER), us=0)
    for c in range(total):
        near[c] = beside(recv[c], -1)
        if c + 1 < total:
            coming = ring(together(sent[c + 1], recv[c])[0], -2 * LAYER)
        waits = [[spread_in], [packed], [home[0]]][min(c, 2)]
        near[c] = together(near[c], *waits, *summed[max(c - 1, 0) : c])[0]
        b1, b2, *own[c] = edges(firsts[c], CHUNKS[c], roles, *inputs, recv[c], near[c])
        from_near = beside(b2, 1)
        if c == 0:
            carry_back, mine = carry(roles, together(carry_recv, b1)[0], spread_in)
            carry_home = arrived(ring(carry_back, 3 * LAYER), us=5)
            b1 = together(b1, carry_back)[0]
        if c + 1 < total:
            recv[c + 1] = arrived(coming, b1)
            from_near = together(from_near, recv[c + 1])[0]
        summed[c] = add(b1, from_near)
        home_sent = summed[c]
        home[c] = ring(summed[c], 2 * LAYER)
        if c == 0:
            home[c] = arrived(home[c])
            packed = ends(together(carry_home, home_sent)[0], mine)
            carried = spread(packed)

    outs = None
    for c in range(total):
        if c:
            home[c] = arrived(home[c], summed[-1], *outs)
        outs = final(firsts[c], CHUNKS[c], roles, own[c], home[c], carried, outs)
    return tuple(outs)


def solution(mesh):
    rows = P(("grp", "seq"), None)
    cols = P(None, ("grp", "seq"))
    return jax.shard_map(
        on_device,
        mesh=mesh,
        in_specs=(rows, rows, rows, rows, cols, cols),
        out_specs=(rows, rows, rows),
        check_vma=False,
    )
```

```python
import functools

import jax
import jax.numpy as jnp
from jax import lax
from jax.experimental import pallas as pl
from jax.experimental.pallas import tpu as pltpu
from jax.sharding import PartitionSpec as P

HEADS = 16
DEPTH = 128
ROWS = 160
AUX = 16
SENT = 2 * ROWS + AUX
BACK = 2 * ROWS
LAYER = 16
UNIT = 2
CHUNKS = (6, 6, 4)
SCALE = DEPTH ** (-0.5)
NT = (((1,), (1,)), ((), ()))
NN = (((1,), (0,)), ((), ()))
TN = (((0,), (0,)), ((), ()))
LIMIT = 60 * 1024 * 1024


def dot(a, b, dims):
    return lax.dot_general(a, b, dims, preferred_element_type=jnp.float32)


def cost(us):
    return pl.CostEstimate(
        flops=int(us * 1.1e9) + 1000, bytes_accessed=int(us * 3.6e6) + 1000, transcendentals=0
    )


def call(body, name, grid=(), us=0, limit=LIMIT, **kwargs):
    return pl.pallas_call(
        body,
        grid=grid,
        compiler_params=pltpu.CompilerParams(vmem_limit_bytes=limit),
        cost_estimate=cost(us),
        name=name,
        **kwargs,
    )


SMEM = pl.BlockSpec(memory_space=pltpu.SMEM)
ANY = pl.BlockSpec(memory_space=pl.ANY)
SMALL = pl.BlockSpec((HEADS, ROWS), lambda i: (0, 0))


def wide(first, unit=UNIT):
    return pl.BlockSpec((ROWS, unit * DEPTH), lambda i: (0, first // unit + i))


def tall(rows, first=0, unit=UNIT):
    return pl.BlockSpec((unit, rows, DEPTH), lambda i: (first // unit + i, 0, 0))


def together(*arrays):
    return lax.optimization_barrier(arrays)


def arrived_kernel(x, out):
    del x, out


def arrived(x, *others, us=100):
    if others:
        x = together(x, *others)[0]
    return call(
        arrived_kernel,
        "arrived",
        us=us,
        limit=16 * 1024 * 1024,
        in_specs=[ANY],
        out_specs=ANY,
        out_shape=jax.ShapeDtypeStruct(x.shape, x.dtype),
        input_output_aliases={0: 0},
    )(x)


def pair(k, v, q, g, lse, delta, mask=None):
    prob = jnp.exp(dot(k, q, NT) * SCALE - lse)
    if mask is not None:
        prob = jnp.where(mask, prob, 0.0)
    dscore = (prob * (dot(v, g, NT) - delta)).astype(jnp.bfloat16)
    prob = prob.astype(jnp.bfloat16)
    return dot(dscore, q, NN) * SCALE, dot(prob, g, NN), dot(dscore, k, TN) * SCALE


def aux_rows(spare, head):
    sub = lax.broadcasted_iota(jnp.int32, (AUX, DEPTH), 0)
    aux = jnp.zeros((AUX, DEPTH), jnp.float32)
    for t in range(2):
        row = spare[t, pl.ds(head, 1), :]
        for piece in range(3):
            part = row.astype(jnp.bfloat16).astype(jnp.float32)
            row = row - part
            for side in range(2):
                at = 6 * t + 2 * piece + side
                aux = jnp.where(sub == at, part[:, side * DEPTH : (side + 1) * DEPTH], aux)
    return aux.astype(jnp.bfloat16)


def read_aux(aux):
    a = aux.astype(jnp.float32)
    rows = []
    for base in (0, 6):
        first = a[base : base + 1] + a[base + 2 : base + 3] + a[base + 4 : base + 5]
        second = a[base + 1 : base + 2] + a[base + 3 : base + 4] + a[base + 5 : base + 6]
        rows.append(jnp.concatenate([first, second[:, : ROWS - DEPTH]], axis=1))
    return rows


def prep_kernel(first, role_at, unit, roles, q, g, k, v, lse, delta, out, spare):
    step = pl.program_id(0)
    spare[...] = jnp.zeros_like(spare)
    spare[0, :, 0:ROWS] = lse[...]
    spare[1, :, 0:ROWS] = delta[...]
    for i in range(unit):
        cols = slice(i * DEPTH, (i + 1) * DEPTH)
        out[i, 2 * ROWS :, :] = aux_rows(spare, first + step * unit + i)

        def put(one, two):
            out[i, 0:ROWS, :] = one[:, cols]
            out[i, ROWS : 2 * ROWS, :] = two[:, cols]

        pl.when(roles[role_at] == 1)(functools.partial(put, q, g))
        pl.when(roles[role_at] == 0)(functools.partial(put, k, v))


def prep(first, count, role_at, roles, q, g, k, v, lse, delta, unit=UNIT):
    return call(
        functools.partial(prep_kernel, first, role_at, unit),
        "prep",
        grid=(count // unit,),
        in_specs=[SMEM] + [wide(first, unit)] * 4 + [SMALL] * 2,
        out_specs=tall(SENT, 0, unit),
        out_shape=jax.ShapeDtypeStruct((count, SENT, DEPTH), jnp.bfloat16),
        scratch_shapes=[pltpu.VMEM((2, HEADS, 2 * DEPTH), jnp.float32)],
    )(roles, q, g, k, v, lse, delta)


def edges_kernel(first, roles, q, g, k, v, lse, delta, one, two, back1, back2, dq, dk, dv):
    step = pl.program_id(0)

    def run(role_b):
        for i in range(UNIT):
            cols = slice(i * DEPTH, (i + 1) * DEPTH)
            head = first + step * UNIT + i
            own_lse, own_delta = lse[pl.ds(head, 1), :], delta[pl.ds(head, 1), :]

            def joined(own, at):
                rows = slice(at * ROWS, (at + 1) * ROWS)
                return jnp.concatenate([own[:, cols], one[i, rows, :], two[i, rows, :]], axis=0)

            if role_b:
                aux = [read_aux(x[i, 2 * ROWS :, :]) for x in (one, two)]
                all_lse = jnp.concatenate([own_lse, aux[0][0], aux[1][0]], axis=1)
                all_delta = jnp.concatenate([own_delta, aux[0][1], aux[1][1]], axis=1)
                shape = (ROWS, 3 * ROWS)
                keys = lax.broadcasted_iota(jnp.int32, shape, 0)
                mask = keys <= lax.broadcasted_iota(jnp.int32, shape, 1)
                key, value, query = pair(
                    k[:, cols], v[:, cols], joined(q, 0), joined(g, 1), all_lse, all_delta, mask
                )
                dk[:, cols] = key.astype(jnp.bfloat16)
                dv[:, cols] = value.astype(jnp.bfloat16)
                query = query.astype(jnp.bfloat16)
                dq[:, cols] = query[0:ROWS]
                for n, back in ((1, back1), (2, back2)):
                    back[i, 0:ROWS, :] = query[n * ROWS : (n + 1) * ROWS]
                    back[i, ROWS:, :] = jnp.zeros((ROWS, DEPTH), jnp.bfloat16)
            else:
                shape = (3 * ROWS, ROWS)
                keys = lax.broadcasted_iota(jnp.int32, shape, 0)
                mask = keys <= lax.broadcasted_iota(jnp.int32, shape, 1)
                mask = jnp.logical_or(mask, keys >= ROWS)
                key, value, query = pair(
                    joined(k, 0), joined(v, 1), q[:, cols], g[:, cols], own_lse, own_delta, mask
                )
                dq[:, cols] = query.astype(jnp.bfloat16)
                key, value = key.astype(jnp.bfloat16), value.astype(jnp.bfloat16)
                dk[:, cols] = key[0:ROWS]
                dv[:, cols] = value[0:ROWS]
                for n, back in ((1, back1), (2, back2)):
                    back[i, 0:ROWS, :] = key[n * ROWS : (n + 1) * ROWS]
                    back[i, ROWS:, :] = value[n * ROWS : (n + 1) * ROWS]

    pl.when(roles[1] == 1)(functools.partial(run, True))
    pl.when(roles[1] == 0)(functools.partial(run, False))


def edges(first, count, roles, q, g, k, v, lse, delta, one, two):
    own = wide(0)
    return call(
        functools.partial(edges_kernel, first),
        "edges",
        limit=24 * 1024 * 1024,
        grid=(count // UNIT,),
        in_specs=[SMEM] + [wide(first)] * 4 + [SMALL] * 2 + [tall(SENT)] * 2,
        out_specs=[tall(BACK)] * 2 + [own] * 3,
        out_shape=[jax.ShapeDtypeStruct((count, BACK, DEPTH), jnp.bfloat16)] * 2
        + [jax.ShapeDtypeStruct((ROWS, count * DEPTH), jnp.bfloat16)] * 3,
    )(roles, q, g, k, v, lse, delta, one, two)


def add_kernel(a, b, out):
    out[...] = (a[...].astype(jnp.float32) + b[...].astype(jnp.float32)).astype(jnp.bfloat16)


def add(a, b):
    vmem = pl.BlockSpec(memory_space=pltpu.VMEM)
    return call(
        add_kernel,
        "add",
        limit=24 * 1024 * 1024,
        in_specs=[vmem] * 2,
        out_specs=vmem,
        out_shape=jax.ShapeDtypeStruct(a.shape, a.dtype),
    )(a, b)


def carry_kernel(roles, recv, held, back, mine):
    layer = roles[3]
    r1, r2 = recv[0:ROWS], recv[ROWS : 2 * ROWS]
    l1, l2 = held[0, 0:ROWS], held[0, ROWS : 2 * ROWS]

    def put(ref, one, two):
        ref[0:ROWS, :] = one.astype(jnp.bfloat16)
        if two is None:
            ref[ROWS:, :] = jnp.zeros((ROWS, DEPTH), jnp.bfloat16)
        else:
            ref[ROWS:, :] = two.astype(jnp.bfloat16)

    @pl.when(layer <= 4)
    def _():
        lse, delta = read_aux(recv[2 * ROWS :])
        key, value, query = pair(l1, l2, r1, r2, lse, delta)
        put(back, query, None)
        put(mine, key, value)

    @pl.when(layer > 4)
    def _():
        lse, delta = read_aux(held[0, 2 * ROWS :])
        key, value, query = pair(r1, r2, l1, l2, lse, delta)
        put(back, key, value)
        put(mine, query, None)


def carry(roles, recv, spread_in):
    out = pl.BlockSpec((BACK, DEPTH), lambda i: (0, 0))
    return call(
        carry_kernel,
        "carry",
        limit=24 * 1024 * 1024,
        grid=(1,),
        in_specs=[
            SMEM,
            pl.BlockSpec((SENT, DEPTH), lambda i: (0, 0)),
            pl.BlockSpec((1, SENT, DEPTH), lambda i: (LAYER - 1, 0, 0)),
        ],
        out_specs=[out] * 2,
        out_shape=[jax.ShapeDtypeStruct((BACK, DEPTH), jnp.bfloat16)] * 2,
    )(roles, recv, spread_in)


def ends_kernel(home, mine, out):
    out[...] = jnp.zeros_like(out)
    out[0] = home[...]
    out[LAYER - 1] = mine[...]


def ends(home, mine):
    vmem = pl.BlockSpec(memory_space=pltpu.VMEM)
    return call(
        ends_kernel,
        "ends",
        limit=48 * 1024 * 1024,
        in_specs=[vmem] * 2,
        out_specs=vmem,
        out_shape=jax.ShapeDtypeStruct((LAYER, BACK, DEPTH), jnp.bfloat16),
    )(home, mine)


def final_kernel(roles, dq, dk, dv, home, carried, *refs):
    oq, ok, ov = refs[-3:]
    layer, place = roles[3], roles[4]
    home_q = layer >= 2
    carried_q = jnp.where(place == 0, layer >= 3, layer >= 5)
    for i in range(UNIT):
        cols = slice(i * DEPTH, (i + 1) * DEPTH)
        f32 = [x[:, cols].astype(jnp.float32) for x in (dq, dk, dv)]
        h1 = home[i, 0:ROWS, :].astype(jnp.float32)
        h2 = home[i, ROWS:, :].astype(jnp.float32)
        c1 = carried[i, 0:ROWS, :].astype(jnp.float32)
        c2 = carried[i, ROWS:, :].astype(jnp.float32)
        to_q = jnp.where(home_q, h1, 0.0) + jnp.where(carried_q, c1, 0.0)
        to_k = jnp.where(home_q, 0.0, h1) + jnp.where(carried_q, 0.0, c1)
        to_v = jnp.where(home_q, 0.0, h2) + jnp.where(carried_q, 0.0, c2)
        oq[:, cols] = (f32[0] + to_q).astype(jnp.bfloat16)
        ok[:, cols] = (f32[1] + to_k).astype(jnp.bfloat16)
        ov[:, cols] = (f32[2] + to_v).astype(jnp.bfloat16)


def final(first, count, roles, own, home, carried, outs):
    held = list(outs) if outs else []
    return call(
        final_kernel,
        "final",
        limit=24 * 1024 * 1024,
        grid=(count // UNIT,),
        in_specs=[SMEM] + [wide(0)] * 3 + [tall(BACK), tall(BACK, first)] + [ANY] * len(held),
        out_specs=[wide(first)] * 3,
        out_shape=[jax.ShapeDtypeStruct((ROWS, HEADS * DEPTH), jnp.bfloat16)] * 3,
        input_output_aliases={6 + n: n for n in range(len(held))},
    )(roles, *own, home, carried, *held)


def on_device(queries, keys, values, out_grad, log_sum, delta):
    count = lax.axis_size("seq")
    position = lax.axis_index("seq")
    layer, place = position // LAYER, position % LAYER
    groups = [list(range(s, s + LAYER)) for s in range(0, count, LAYER)]
    inputs = (queries, out_grad, keys, values, log_sum, delta)

    def ring(x, by):
        return lax.ppermute(x, "seq", [(i, (i + by) % count) for i in range(count)])

    def beside(x, by):
        pairs = [(i, i + by) for i in range(count) if (i + by) // LAYER == i // LAYER]
        return lax.ppermute(x, "seq", pairs)

    def spread(x):
        return lax.all_to_all(x, "seq", 0, 0, axis_index_groups=groups, tiled=True)

    carry_q = jnp.where(place == LAYER - 1, layer >= 5, layer >= 3)
    roles = jnp.stack([layer >= 2, layer <= 5, carry_q, layer, place]).astype(jnp.int32)
    firsts = [sum(CHUNKS[:n]) for n in range(len(CHUNKS))]
    total = len(CHUNKS)

    sent = [None] * total
    sent[0] = prep(firsts[0], CHUNKS[0], 0, roles, *inputs)
    roles1 = together(roles, sent[0])[0]
    spread_in = spread(prep(0, HEADS, 2, roles1, *inputs, unit=4))
    for c in range(1, total):
        sent[c] = prep(firsts[c], CHUNKS[c], 0, roles1, *inputs)

    recv, near, own, summed, home = ([None] * total for _ in range(5))
    carried = carry_back = packed = None
    recv[0] = arrived(ring(sent[0], -2 * LAYER), *sent[1:])
    carry_recv = arrived(ring(spread_in[0], -3 * LAYER), us=0)
    for c in range(total):
        near[c] = beside(recv[c], -1)
        if c + 1 < total:
            coming = ring(together(sent[c + 1], recv[c])[0], -2 * LAYER)
        waits = [[spread_in], [packed], [home[0]]][min(c, 2)]
        near[c] = together(near[c], *waits, *summed[max(c - 1, 0) : c])[0]
        b1, b2, *own[c] = edges(firsts[c], CHUNKS[c], roles, *inputs, recv[c], near[c])
        from_near = beside(b2, 1)
        if c == 0:
            carry_back, mine = carry(roles, together(carry_recv, b1)[0], spread_in)
            carry_home = arrived(ring(carry_back, 3 * LAYER), us=5)
            b1 = together(b1, carry_back)[0]
        if c + 1 < total:
            recv[c + 1] = arrived(coming, b1)
            from_near = together(from_near, recv[c + 1])[0]
        summed[c] = add(b1, from_near)
        home_sent = summed[c]
        home[c] = ring(summed[c], 2 * LAYER)
        if c == 0:
            home[c] = arrived(home[c])
            packed = ends(together(carry_home, home_sent)[0], mine)
            carried = spread(packed)

    outs = None
    for c in range(total):
        if c:
            home[c] = arrived(home[c], summed[-1], *outs)
        outs = final(firsts[c], CHUNKS[c], roles, own[c], home[c], carried, outs)
    return tuple(outs)


def solution(mesh):
    rows = P(("grp", "seq"), None)
    cols = P(None, ("grp", "seq"))
    return jax.shard_map(
        on_device,
        mesh=mesh,
        in_specs=(rows, rows, rows, rows, cols, cols),
        out_specs=(rows, rows, rows),
        check_vma=False,
    )
```

```python
import functools

import jax
import jax.numpy as jnp
from jax import lax
from jax.experimental import pallas as pl
from jax.experimental.pallas import tpu as pltpu
from jax.sharding import PartitionSpec as P

HEADS = 16
DEPTH = 128
ROWS = 160
AUX = 16
SENT = 2 * ROWS + AUX
BACK = 2 * ROWS
LAYER = 16
UNIT = 2
CHUNKS = (6, 6, 4)
SCALE = DEPTH ** (-0.5)
NT = (((1,), (1,)), ((), ()))
NN = (((1,), (0,)), ((), ()))
TN = (((0,), (0,)), ((), ()))
LIMIT = 60 * 1024 * 1024


def dot(a, b, dims):
    return lax.dot_general(a, b, dims, preferred_element_type=jnp.float32)


def cost(us):
    return pl.CostEstimate(
        flops=int(us * 1.1e9) + 1000, bytes_accessed=int(us * 3.6e6) + 1000, transcendentals=0
    )


def call(body, name, grid=(), us=0, limit=LIMIT, **kwargs):
    return pl.pallas_call(
        body,
        grid=grid,
        compiler_params=pltpu.CompilerParams(vmem_limit_bytes=limit),
        cost_estimate=cost(us),
        name=name,
        **kwargs,
    )


SMEM = pl.BlockSpec(memory_space=pltpu.SMEM)
ANY = pl.BlockSpec(memory_space=pl.ANY)
SMALL = pl.BlockSpec((HEADS, ROWS), lambda i: (0, 0))


def wide(first, unit=UNIT):
    return pl.BlockSpec((ROWS, unit * DEPTH), lambda i: (0, first // unit + i))


def tall(rows, first=0, unit=UNIT):
    return pl.BlockSpec((unit, rows, DEPTH), lambda i: (first // unit + i, 0, 0))


def together(*arrays):
    return lax.optimization_barrier(arrays)


def arrived_kernel(x, out):
    del x, out


def arrived(x, *others, us=100):
    if others:
        x = together(x, *others)[0]
    return call(
        arrived_kernel,
        "arrived",
        us=us,
        limit=16 * 1024 * 1024,
        in_specs=[ANY],
        out_specs=ANY,
        out_shape=jax.ShapeDtypeStruct(x.shape, x.dtype),
        input_output_aliases={0: 0},
    )(x)


def pair(k, v, q, g, lse, delta, mask=None):
    prob = jnp.exp(dot(k, q, NT) * SCALE - lse)
    if mask is not None:
        prob = jnp.where(mask, prob, 0.0)
    dscore = (prob * (dot(v, g, NT) - delta)).astype(jnp.bfloat16)
    prob = prob.astype(jnp.bfloat16)
    return dot(dscore, q, NN) * SCALE, dot(prob, g, NN), dot(dscore, k, TN) * SCALE


def aux_rows(spare, head):
    sub = lax.broadcasted_iota(jnp.int32, (AUX, DEPTH), 0)
    aux = jnp.zeros((AUX, DEPTH), jnp.float32)
    for t in range(2):
        row = spare[t, pl.ds(head, 1), :]
        for piece in range(3):
            part = row.astype(jnp.bfloat16).astype(jnp.float32)
            row = row - part
            for side in range(2):
                at = 6 * t + 2 * piece + side
                aux = jnp.where(sub == at, part[:, side * DEPTH : (side + 1) * DEPTH], aux)
    return aux.astype(jnp.bfloat16)


def read_aux(aux):
    a = aux.astype(jnp.float32)
    rows = []
    for base in (0, 6):
        first = a[base : base + 1] + a[base + 2 : base + 3] + a[base + 4 : base + 5]
        second = a[base + 1 : base + 2] + a[base + 3 : base + 4] + a[base + 5 : base + 6]
        rows.append(jnp.concatenate([first, second[:, : ROWS - DEPTH]], axis=1))
    return rows


def prep_kernel(first, role_at, unit, roles, q, g, k, v, lse, delta, out, spare):
    step = pl.program_id(0)
    spare[...] = jnp.zeros_like(spare)
    spare[0, :, 0:ROWS] = lse[...]
    spare[1, :, 0:ROWS] = delta[...]
    for i in range(unit):
        cols = slice(i * DEPTH, (i + 1) * DEPTH)
        out[i, 2 * ROWS :, :] = aux_rows(spare, first + step * unit + i)

        def put(one, two):
            out[i, 0:ROWS, :] = one[:, cols]
            out[i, ROWS : 2 * ROWS, :] = two[:, cols]

        pl.when(roles[role_at] == 1)(functools.partial(put, q, g))
        pl.when(roles[role_at] == 0)(functools.partial(put, k, v))


def prep(first, count, role_at, roles, q, g, k, v, lse, delta, unit=UNIT):
    return call(
        functools.partial(prep_kernel, first, role_at, unit),
        "prep",
        grid=(count // unit,),
        in_specs=[SMEM] + [wide(first, unit)] * 4 + [SMALL] * 2,
        out_specs=tall(SENT, 0, unit),
        out_shape=jax.ShapeDtypeStruct((count, SENT, DEPTH), jnp.bfloat16),
        scratch_shapes=[pltpu.VMEM((2, HEADS, 2 * DEPTH), jnp.float32)],
    )(roles, q, g, k, v, lse, delta)


def edges_kernel(first, roles, q, g, k, v, lse, delta, one, two, back1, back2, dq, dk, dv):
    step = pl.program_id(0)

    def run(role_b):
        for i in range(UNIT):
            cols = slice(i * DEPTH, (i + 1) * DEPTH)
            head = first + step * UNIT + i
            own_lse, own_delta = lse[pl.ds(head, 1), :], delta[pl.ds(head, 1), :]

            def joined(own, at):
                rows = slice(at * ROWS, (at + 1) * ROWS)
                return jnp.concatenate([own[:, cols], one[i, rows, :], two[i, rows, :]], axis=0)

            if role_b:
                aux = [read_aux(x[i, 2 * ROWS :, :]) for x in (one, two)]
                all_lse = jnp.concatenate([own_lse, aux[0][0], aux[1][0]], axis=1)
                all_delta = jnp.concatenate([own_delta, aux[0][1], aux[1][1]], axis=1)
                shape = (ROWS, 3 * ROWS)
                keys = lax.broadcasted_iota(jnp.int32, shape, 0)
                mask = keys <= lax.broadcasted_iota(jnp.int32, shape, 1)
                key, value, query = pair(
                    k[:, cols], v[:, cols], joined(q, 0), joined(g, 1), all_lse, all_delta, mask
                )
                dk[:, cols] = key.astype(jnp.bfloat16)
                dv[:, cols] = value.astype(jnp.bfloat16)
                query = query.astype(jnp.bfloat16)
                dq[:, cols] = query[0:ROWS]
                for n, back in ((1, back1), (2, back2)):
                    back[i, 0:ROWS, :] = query[n * ROWS : (n + 1) * ROWS]
                    back[i, ROWS:, :] = jnp.zeros((ROWS, DEPTH), jnp.bfloat16)
            else:
                shape = (3 * ROWS, ROWS)
                keys = lax.broadcasted_iota(jnp.int32, shape, 0)
                mask = keys <= lax.broadcasted_iota(jnp.int32, shape, 1)
                mask = jnp.logical_or(mask, keys >= ROWS)
                key, value, query = pair(
                    joined(k, 0), joined(v, 1), q[:, cols], g[:, cols], own_lse, own_delta, mask
                )
                dq[:, cols] = query.astype(jnp.bfloat16)
                key, value = key.astype(jnp.bfloat16), value.astype(jnp.bfloat16)
                dk[:, cols] = key[0:ROWS]
                dv[:, cols] = value[0:ROWS]
                for n, back in ((1, back1), (2, back2)):
                    back[i, 0:ROWS, :] = key[n * ROWS : (n + 1) * ROWS]
                    back[i, ROWS:, :] = value[n * ROWS : (n + 1) * ROWS]

    pl.when(roles[1] == 1)(functools.partial(run, True))
    pl.when(roles[1] == 0)(functools.partial(run, False))


def edges(first, count, roles, q, g, k, v, lse, delta, one, two):
    own = wide(0)
    return call(
        functools.partial(edges_kernel, first),
        "edges",
        limit=24 * 1024 * 1024,
        grid=(count // UNIT,),
        in_specs=[SMEM] + [wide(first)] * 4 + [SMALL] * 2 + [tall(SENT)] * 2,
        out_specs=[tall(BACK)] * 2 + [own] * 3,
        out_shape=[jax.ShapeDtypeStruct((count, BACK, DEPTH), jnp.bfloat16)] * 2
        + [jax.ShapeDtypeStruct((ROWS, count * DEPTH), jnp.bfloat16)] * 3,
    )(roles, q, g, k, v, lse, delta, one, two)


def add_kernel(a, b, out):
    out[...] = (a[...].astype(jnp.float32) + b[...].astype(jnp.float32)).astype(jnp.bfloat16)


def add(a, b):
    vmem = pl.BlockSpec(memory_space=pltpu.VMEM)
    return call(
        add_kernel,
        "add",
        limit=24 * 1024 * 1024,
        in_specs=[vmem] * 2,
        out_specs=vmem,
        out_shape=jax.ShapeDtypeStruct(a.shape, a.dtype),
    )(a, b)


def carry_kernel(roles, recv, held, back, mine):
    layer = roles[3]
    r1, r2 = recv[0:ROWS], recv[ROWS : 2 * ROWS]
    l1, l2 = held[0, 0:ROWS], held[0, ROWS : 2 * ROWS]

    def put(ref, one, two):
        ref[0:ROWS, :] = one.astype(jnp.bfloat16)
        if two is None:
            ref[ROWS:, :] = jnp.zeros((ROWS, DEPTH), jnp.bfloat16)
        else:
            ref[ROWS:, :] = two.astype(jnp.bfloat16)

    @pl.when(layer <= 4)
    def _():
        lse, delta = read_aux(recv[2 * ROWS :])
        key, value, query = pair(l1, l2, r1, r2, lse, delta)
        put(back, query, None)
        put(mine, key, value)

    @pl.when(layer > 4)
    def _():
        lse, delta = read_aux(held[0, 2 * ROWS :])
        key, value, query = pair(r1, r2, l1, l2, lse, delta)
        put(back, key, value)
        put(mine, query, None)


def carry(roles, recv, spread_in):
    out = pl.BlockSpec((BACK, DEPTH), lambda i: (0, 0))
    return call(
        carry_kernel,
        "carry",
        limit=24 * 1024 * 1024,
        grid=(1,),
        in_specs=[
            SMEM,
            pl.BlockSpec((SENT, DEPTH), lambda i: (0, 0)),
            pl.BlockSpec((1, SENT, DEPTH), lambda i: (LAYER - 1, 0, 0)),
        ],
        out_specs=[out] * 2,
        out_shape=[jax.ShapeDtypeStruct((BACK, DEPTH), jnp.bfloat16)] * 2,
    )(roles, recv, spread_in)


def ends_kernel(home, mine, out):
    out[...] = jnp.zeros_like(out)
    out[0] = home[...]
    out[LAYER - 1] = mine[...]


def ends(home, mine):
    vmem = pl.BlockSpec(memory_space=pltpu.VMEM)
    return call(
        ends_kernel,
        "ends",
        limit=48 * 1024 * 1024,
        in_specs=[vmem] * 2,
        out_specs=vmem,
        out_shape=jax.ShapeDtypeStruct((LAYER, BACK, DEPTH), jnp.bfloat16),
    )(home, mine)


def final_kernel(roles, dq, dk, dv, home, carried, *refs):
    oq, ok, ov = refs[-3:]
    layer, place = roles[3], roles[4]
    home_q = layer >= 2
    carried_q = jnp.where(place == 0, layer >= 3, layer >= 5)
    for i in range(UNIT):
        cols = slice(i * DEPTH, (i + 1) * DEPTH)
        f32 = [x[:, cols].astype(jnp.float32) for x in (dq, dk, dv)]
        h1 = home[i, 0:ROWS, :].astype(jnp.float32)
        h2 = home[i, ROWS:, :].astype(jnp.float32)
        c1 = carried[i, 0:ROWS, :].astype(jnp.float32)
        c2 = carried[i, ROWS:, :].astype(jnp.float32)
        to_q = jnp.where(home_q, h1, 0.0) + jnp.where(carried_q, c1, 0.0)
        to_k = jnp.where(home_q, 0.0, h1) + jnp.where(carried_q, 0.0, c1)
        to_v = jnp.where(home_q, 0.0, h2) + jnp.where(carried_q, 0.0, c2)
        oq[:, cols] = (f32[0] + to_q).astype(jnp.bfloat16)
        ok[:, cols] = (f32[1] + to_k).astype(jnp.bfloat16)
        ov[:, cols] = (f32[2] + to_v).astype(jnp.bfloat16)


def final(first, count, roles, own, home, carried, outs):
    held = list(outs) if outs else []
    return call(
        final_kernel,
        "final",
        limit=24 * 1024 * 1024,
        grid=(count // UNIT,),
        in_specs=[SMEM] + [wide(0)] * 3 + [tall(BACK), tall(BACK, first)] + [ANY] * len(held),
        out_specs=[wide(first)] * 3,
        out_shape=[jax.ShapeDtypeStruct((ROWS, HEADS * DEPTH), jnp.bfloat16)] * 3,
        input_output_aliases={6 + n: n for n in range(len(held))},
    )(roles, *own, home, carried, *held)


def on_device(queries, keys, values, out_grad, log_sum, delta):
    count = lax.axis_size("seq")
    position = lax.axis_index("seq")
    layer, place = position // LAYER, position % LAYER
    groups = [list(range(s, s + LAYER)) for s in range(0, count, LAYER)]
    inputs = (queries, out_grad, keys, values, log_sum, delta)

    def ring(x, by):
        return lax.ppermute(x, "seq", [(i, (i + by) % count) for i in range(count)])

    def beside(x, by):
        pairs = [(i, i + by) for i in range(count) if (i + by) // LAYER == i // LAYER]
        return lax.ppermute(x, "seq", pairs)

    def spread(x):
        return lax.all_to_all(x, "seq", 0, 0, axis_index_groups=groups, tiled=True)

    carry_q = jnp.where(place == LAYER - 1, layer >= 5, layer >= 3)
    roles = jnp.stack([layer >= 2, layer <= 5, carry_q, layer, place]).astype(jnp.int32)
    firsts = [sum(CHUNKS[:n]) for n in range(len(CHUNKS))]
    total = len(CHUNKS)

    sent = [None] * total
    sent[0] = prep(firsts[0], CHUNKS[0], 0, roles, *inputs, unit=CHUNKS[0])
    roles1 = together(roles, sent[0])[0]
    spread_in = spread(prep(0, HEADS, 2, roles1, *inputs, unit=8))
    for c in range(1, total):
        sent[c] = prep(firsts[c], CHUNKS[c], 0, roles1, *inputs, unit=CHUNKS[c])

    recv, near, own, summed, home = ([None] * total for _ in range(5))
    carried = carry_back = packed = None
    recv[0] = arrived(ring(sent[0], -2 * LAYER), *sent[1:])
    carry_recv = arrived(ring(spread_in[0], -3 * LAYER), us=0)
    for c in range(total):
        near[c] = beside(recv[c], -1)
        if c + 1 < total:
            coming = ring(together(sent[c + 1], recv[c])[0], -2 * LAYER)
        waits = [[spread_in], [packed], [home[0]]][min(c, 2)]
        near[c] = together(near[c], *waits, *summed[max(c - 1, 0) : c])[0]
        b1, b2, *own[c] = edges(firsts[c], CHUNKS[c], roles, *inputs, recv[c], near[c])
        from_near = beside(b2, 1)
        if c == 0:
            carry_back, mine = carry(roles, together(carry_recv, b1)[0], spread_in)
            carry_home = arrived(ring(carry_back, 3 * LAYER), us=5)
            b1 = together(b1, carry_back)[0]
        if c + 1 < total:
            recv[c + 1] = arrived(coming, b1)
            from_near = together(from_near, recv[c + 1])[0]
        summed[c] = add(b1, from_near)
        home_sent = summed[c]
        home[c] = ring(summed[c], 2 * LAYER)
        if c == 0:
            home[c] = arrived(home[c])
            packed = ends(together(carry_home, home_sent)[0], mine)
            carried = spread(packed)

    outs = None
    for c in range(total):
        if c:
            home[c] = arrived(home[c], summed[-1], *outs)
        outs = final(firsts[c], CHUNKS[c], roles, own[c], home[c], carried, outs)
    return tuple(outs)


def solution(mesh):
    rows = P(("grp", "seq"), None)
    cols = P(None, ("grp", "seq"))
    return jax.shard_map(
        on_device,
        mesh=mesh,
        in_specs=(rows, rows, rows, rows, cols, cols),
        out_specs=(rows, rows, rows),
        check_vma=False,
    )
```
